32 devices in a mesh: section: 4 (over y, x), expert: 8 (over z, core).
Axes of the slice: x: 2, y: 2, z: 4, core: 2. Of those that a mesh axis runs over, the one named last changes fastest.
Arguments:
- section_inputs: bfloat16 [4, 3, 512, 2048], P('section', None, 'expert'), may hold values from -6 to 6
- cotangent: bfloat16 [3, 512, 2048], P(None, 'expert'), may hold values from -6 to 6
- expert_ids: int32 [4, 3, 512, 2], P('section', None, 'expert'), may hold values from 0 to 7, all different within a row; in each aligned block of 64 rows (0 to 63, 64 to 127, ..., all dimensions but the last counted through in order) at most 24 rows name the same one
- route_weights: float32 [4, 3, 512, 2], P('section', None, 'expert'), may hold values from 0.2 to 1
- w_gate: bfloat16 [4, 8, 2048, 512], P('section', 'expert'), may hold values from -0.125 to 0.125
- w_up: bfloat16 [4, 8, 2048, 512], P('section', 'expert'), may hold values from -0.125 to 0.125
- w_down: bfloat16 [4, 8, 512, 2048], P('section', 'expert'), may hold values from -0.25 to 0.25
Outputs:
- input_grads: bfloat16 [4, 3, 512, 2048], P('section', None, 'expert')
- grad_gate: float32 [4, 8, 2048, 512], P('section', 'expert')
- grad_up: float32 [4, 8, 2048, 512], P('section', 'expert')
- precond_down: float32 [4, 8, 512, 2048], P('section', 'expert')
The draws below stay inside these ranges and needn't reach their ends.
Inputs may be any that keep to these rules, and one draw needn't show every extreme that they name: `expert_ids`: each token names two different experts. In each aligned block of 64 rows (the rows of one device in one layer and micro-batch) no expert is named by more than 24 rows, a bound that some block reaches.
All inputs are finite; a program needn't handle non-finite values.
Results may differ from the reference program's by a relative error of at most 0.013.
Values may be sent and summed in bfloat16 or wider, within the bound.
A program may use at most 192 MiB of HBM per device.

```python
import math
import jax
import jax.numpy as jnp
import numpy as np
from jax import lax

D = 2048
FF_E = 512
ROWS_DEV = 64
TICKS = 3
NS_ITERS = 5
LAYERS = 4
EXPERTS = 8
TOKENS = 512
CAP = 24
N_EXPERT = 8


def block_levels(key, extent, pieces, smallest, largest):
    def one(axis_at, parts):
        steps = jax.random.uniform(jax.random.fold_in(jax.random.fold_in(key, 6), axis_at), (parts,), jnp.float32, smallest / len(pieces), largest / len(pieces))
        return jnp.repeat(jnp.exp(steps), extent[axis_at] // parts).reshape((-1,) + (1,) * (len(extent) - axis_at - 1))

    loudness = one(*pieces[0])
    for cut in pieces[1:]:
        loudness = loudness * one(*cut)
    return loudness


def assign_block(stream_key, own, number, rows, number_of, top, reach, lean):
    order = jax.random.permutation(stream_key, number_of)
    crowded, ordinary = portions_of(number_of, rows * top, reach, lean, True), portions_of(number_of, rows * top, reach, lean, False)
    places = jnp.arange(number_of)

    def named(tallies, turn):
        used = int((tallies > 0).sum())
        fixed = max(1, used // 4)
        shifted = fixed + (places - fixed + turn * (used - fixed)) % max(1, number_of - fixed)
        return jnp.zeros((number_of,), jnp.int32).at[order[jnp.where(places < fixed, places, shifted)]].set(jnp.asarray(tallies, jnp.int32))

    tallies = jnp.where(number % 4 == 0, named(crowded, number // 4), named(ordinary, number - number // 4 - 1))
    mixed = jax.random.permutation(jax.random.fold_in(own, 3), number_of)
    donor, receiver = mixed[0:number_of // 2 * 2:2], mixed[1:number_of // 2 * 2:2]
    margin = jnp.minimum(tallies[donor] - 1, reach - tallies[receiver]) // 2
    margin = jnp.where((donor == order[0]) | (receiver == order[0]) | (tallies[receiver] == 0), 0, jnp.maximum(margin, 0))
    shifted = jax.random.randint(jax.random.fold_in(own, 4), (number_of // 2,), 0, 1 << 20) % (margin + 1)
    tallies = tallies.at[donor].add(-shifted).at[receiver].add(shifted)
    members = jnp.searchsorted(jnp.cumsum(tallies), jnp.arange(rows * top), side="right").astype(jnp.int32)
    grid = members.reshape(top, rows).T
    grid = grid[jax.random.permutation(jax.random.fold_in(own, 1), rows)]
    turn = jax.random.randint(jax.random.fold_in(own, 2), (rows, 1), 0, top)
    return jnp.take_along_axis(grid, (jnp.arange(top)[None, :] + turn) % top, axis=1)


def portions_of(count, total, bound, lean, full):
    loads = [(1 << 20) // math.isqrt(grade ** lean) + 1 for grade in range(1, count + 1)]
    largest = bound if full else min(bound, max(-(-total // count), total * loads[0] // sum(loads)))
    least = 1 if total - largest >= count - 1 else 0
    given, spare = [largest] + [least] * (count - 1), total - largest - least * (count - 1)
    while spare > 0:
        free = [i for i in range(1, count) if given[i] < largest] or [i for i in range(1, count) if given[i] < bound]
        mass, left = sum([loads[i] for i in free]), spare
        for i in free:
            addition = min(bound - given[i], max(1, left * loads[i] // mass), spare)
            given[i] = given[i] + addition
            spare = spare - addition
    return np.array(given)


def gaussian(rng, dims, spread, limit, split=(), kind=jnp.bfloat16):
    gain = block_levels(rng, dims, split, -0.22, 0.18) if split else 1.0
    values = jax.random.normal(rng, dims, jnp.float32) * spread * gain
    return jnp.minimum(jnp.maximum(values, -limit), limit).astype(kind)


def setup_inputs(seed: int = 0) -> dict:
    key_list = jax.random.split(jax.random.key(seed), 8)
    section_inputs = gaussian(key_list[0], (LAYERS, TICKS, TOKENS, D), 1.0, 6.0, ((0, 4), (2, 8)))
    cotangent = gaussian(key_list[1], (TICKS, TOKENS, D), 1.0, 6.0, ((1, 8),))
    expert_ids_keys = jax.random.split(jax.random.fold_in(key_list[2], 1), LAYERS * TICKS * TOKENS // ROWS_DEV)
    expert_ids_turns = jax.random.permutation(jax.random.fold_in(key_list[2], 3), LAYERS * TICKS * TOKENS // ROWS_DEV)
    expert_ids = jax.vmap(lambda own, number: assign_block(jax.random.fold_in(key_list[2], 2), own, number, ROWS_DEV, EXPERTS, 2, CAP, 2))(expert_ids_keys, expert_ids_turns).reshape((LAYERS, TICKS, TOKENS, 2))
    route_weights = jnp.clip(0.2 + 0.8 * jax.random.uniform(key_list[3], (LAYERS, TICKS, TOKENS, 2), jnp.float32) ** block_levels(key_list[3], (LAYERS, TICKS, TOKENS, 2), ((0, 4), (2, 8)), -0.2, 0.2), 0.2, 1.0)
    w_gate = gaussian(key_list[4], (LAYERS, EXPERTS, D, FF_E), D ** -0.5, 0.125, ((0, 4), (1, 8)))
    w_up = gaussian(key_list[5], (LAYERS, EXPERTS, D, FF_E), D ** -0.5, 0.125, ((0, 4), (1, 8)))
    w_down = gaussian(key_list[6], (LAYERS, EXPERTS, FF_E, D), FF_E ** -0.5, 0.25, ((0, 4), (1, 8)))
    return dict(section_inputs=section_inputs, cotangent=cotangent, expert_ids=expert_ids, route_weights=route_weights, w_gate=w_gate, w_up=w_up, w_down=w_down)


damping = 0.1
epsilon = 1e-06

def silu_slope(values):
    logistic = jax.nn.sigmoid(values)
    return logistic * (1.0 + values * (1.0 - logistic))

def inverse_root(curvature, iterations):
    identity_m = jnp.eye(curvature.shape[0], dtype=jnp.float32)
    frobenius = jnp.sqrt(jnp.sum(curvature * curvature))
    current = curvature / frobenius
    result = identity_m * frobenius ** (-0.25)
    for turn_index in range(iterations):
        factor = (5.0 * identity_m - current) * 0.25
        result = jnp.dot(result, factor, precision=lax.Precision.HIGHEST)
        square = jnp.dot(factor, factor, precision=lax.Precision.HIGHEST)
        fourth = jnp.dot(square, square, precision=lax.Precision.HIGHEST)
        current = jnp.dot(fourth, current, precision=lax.Precision.HIGHEST)
    return result

def reference(section_inputs, cotangent, expert_ids, route_weights, w_gate, w_up, w_down):
    f32 = jnp.float32
    bf16 = jnp.bfloat16
    slots_all = N_EXPERT * CAP
    cots = [cotangent[tick_index] for tick_index in range(TICKS)]
    grads_in = [[None] * TICKS for layer_index in range(LAYERS)]
    gate_list = [None] * LAYERS
    up_list = [None] * LAYERS
    pre_list = [None] * LAYERS
    for layer in reversed(range(LAYERS)):
        weight_gate = w_gate[layer].astype(f32)
        weight_up = w_up[layer].astype(f32)
        weight_down = w_down[layer].astype(f32)
        acc_gate = jnp.zeros((EXPERTS, D, FF_E), f32)
        acc_up = jnp.zeros((EXPERTS, D, FF_E), f32)
        acc_down = jnp.zeros((EXPERTS, FF_E, D), f32)
        acc_gram = jnp.zeros((EXPERTS, FF_E, FF_E), f32)
        for tick in range(TICKS):
            current_cot = cots[tick]
            flat_ids = expert_ids[layer, tick].reshape(N_EXPERT, ROWS_DEV * 2)
            onehot = (flat_ids[:, :, None] == jnp.arange(EXPERTS, dtype=jnp.int32)[None, None, :]).astype(jnp.int32)
            ranking = lax.optimization_barrier(jnp.sum((jnp.cumsum(onehot, axis=1) - onehot) * onehot, axis=2))
            slot = (jnp.arange(N_EXPERT, dtype=jnp.int32)[:, None] * CAP + ranking).astype(jnp.int32)
            rows_x = jnp.repeat(section_inputs[layer, tick], 2, axis=0).reshape(N_EXPERT, ROWS_DEV * 2, D)
            scaled = (route_weights[layer, tick][:, :, None] * current_cot.astype(f32)[:, None, :]).astype(bf16)
            scaled = scaled.reshape(N_EXPERT, ROWS_DEV * 2, D)
            buf_x = jnp.zeros((EXPERTS, slots_all, D), bf16).at[flat_ids, slot].set(rows_x)
            buf_g = jnp.zeros((EXPERTS, slots_all, D), bf16).at[flat_ids, slot].set(scaled)
            xs32 = buf_x.astype(f32)
            gs32 = buf_g.astype(f32)
            gate = jnp.einsum('esd,edf->esf', xs32, weight_gate)
            up_proj = jnp.einsum('esd,edf->esf', xs32, weight_up)
            soft_gate = jax.nn.silu(gate)
            hidden = (soft_gate * up_proj).astype(bf16)
            grad_hidden = jnp.einsum('esd,efd->esf', gs32, weight_down)
            d_gate = (grad_hidden * up_proj * silu_slope(gate)).astype(bf16)
            d_up = (grad_hidden * soft_gate).astype(bf16)
            dg32 = d_gate.astype(f32)
            du32 = d_up.astype(f32)
            hid32 = hidden.astype(f32)
            expert_back = (jnp.einsum('esf,edf->esd', dg32, weight_gate) + jnp.einsum('esf,edf->esd', du32, weight_up)).astype(bf16)
            acc_gate = acc_gate + jnp.einsum('esd,esf->edf', xs32, dg32)
            acc_up = acc_up + jnp.einsum('esd,esf->edf', xs32, du32)
            acc_down = acc_down + jnp.einsum('esf,esd->efd', hid32, gs32)
            acc_gram = acc_gram + jnp.einsum('esf,esg->efg', hid32, hid32)
            back = expert_back[flat_ids, slot].astype(f32).reshape(TOKENS, 2, D).sum(axis=1)
            new_cot = (current_cot.astype(f32) + back).astype(bf16)
            grads_in[layer][tick] = new_cot
            cots[tick] = new_cot
        traces = jnp.trace(acc_gram, axis1=1, axis2=2)[:, None, None]
        curvature = acc_gram * (FF_E / (traces + epsilon)) + damping * jnp.eye(FF_E, dtype=f32)[None]
        roots = jax.vmap(lambda matrix: inverse_root(matrix, NS_ITERS))(curvature)
        pre_list[layer] = jnp.matmul(roots, acc_down, precision=lax.Precision.HIGHEST)
        gate_list[layer] = acc_gate
        up_list[layer] = acc_up
    input_grads = jnp.stack([jnp.stack(grads_in[layer_index]) for layer_index in range(LAYERS)])
    return (input_grads, jnp.stack(gate_list), jnp.stack(up_list), jnp.stack(pre_list))
```

```python
import jax
import jax.numpy as jnp
from jax import lax
from jax.sharding import PartitionSpec as P

NS_ITERS = 5


damping = 0.1
epsilon = 1e-06


def from_behind(value, axis, steps):
    count = lax.axis_size(axis)
    leading, last = (max(0, -steps), min(count, count - steps))
    return lax.ppermute(value, axis, [(source, source + steps) for source in range(leading, last)])


def silu_slope(values):
    logistic = jax.nn.sigmoid(values)
    return logistic * (1.0 + values * (1.0 - logistic))


def contract(former, latter, former_dim, latter_dim):
    return lax.dot_general(
        former,
        latter,
        (((former_dim,), (latter_dim,)), ((), ())),
        preferred_element_type=jnp.float32,
    )


def inverse_root(curvature, iterations):
    bf16 = jnp.bfloat16

    def product(former, latter):
        return jnp.dot(former.astype(bf16), latter.astype(bf16), preferred_element_type=jnp.float32)

    identity_m = jnp.eye(curvature.shape[0], dtype=jnp.float32)
    frobenius = jnp.sqrt(jnp.sum(curvature * curvature))
    current = curvature / frobenius
    start = frobenius ** (-0.25)
    result = start * (1.25 * identity_m - 0.25 * current)
    for turn_index in range(1, iterations):
        low = 0.0625 * product(current, current) - 0.625 * current
        high = 3.125 * low + product(low, low)
        current = 2.44140625 * current + product(high, current)
        result = 1.25 * result - 0.25 * product(result, current)
    return result


def slot_tables(tick_ids, experts, capacity):
    flat_ids = tick_ids.reshape(-1)
    index = jnp.arange(flat_ids.shape[0], dtype=jnp.int32)
    earlier = (flat_ids[:, None] == flat_ids[None, :]) & (index[None, :] < index[:, None])
    ranking = jnp.sum(earlier.astype(jnp.int32), axis=1)
    target = flat_ids * capacity + ranking
    places = jnp.arange(experts * capacity, dtype=jnp.int32)
    chosen = (places[:, None] == target[None, :]).astype(jnp.int32)
    by_row = chosen.reshape(experts * capacity, -1, 2).sum(axis=2)
    return (
        chosen.astype(jnp.bfloat16).reshape(experts, capacity, -1),
        by_row.astype(jnp.bfloat16).reshape(experts, capacity, -1),
    )


def expert_backward(rows_g, gate, up_proj, weight_gate, weight_up, weight_down):
    soft_gate = jax.nn.silu(gate)
    grad_hidden = contract(rows_g, weight_down, 1, 1)
    d_gate = (grad_hidden * up_proj * silu_slope(gate)).astype(jnp.bfloat16)
    d_up = (grad_hidden * soft_gate).astype(jnp.bfloat16)
    back_rows = (contract(d_gate, weight_gate, 1, 1) + contract(d_up, weight_up, 1, 1)).astype(
        jnp.bfloat16
    )
    return (back_rows, d_gate, d_up)


def shards(section_inputs, cotangent, expert_ids, route_weights, w_gate, w_up, w_down):
    f32 = jnp.float32
    bf16 = jnp.bfloat16
    section = lax.axis_index("section")
    sections = lax.axis_size("section")
    experts = lax.axis_size("expert")
    ticks = section_inputs.shape[1]
    rows = section_inputs.shape[2]
    width = section_inputs.shape[3]
    capacity = max(2, 3 * rows // experts)
    weight_gate = w_gate[0, 0]
    weight_up = w_up[0, 0]
    weight_down = w_down[0, 0]
    hidden_width = weight_gate.shape[1]
    inputs_here = section_inputs[0]
    choices_here = expert_ids[0]
    scales_here = route_weights[0]
    results = jnp.zeros_like(inputs_here)
    incoming = jnp.zeros((rows, width), bf16)
    tables = jax.vmap(lambda tick_ids: slot_tables(tick_ids, experts, capacity))(choices_here)
    packed = jnp.einsum(
        "tncr,trd->ntcd", tables[1], inputs_here, preferred_element_type=f32
    ).astype(bf16)
    held = lax.all_to_all(packed, "expert", split_axis=0, concat_axis=0, tiled=True)
    held_rows = held.reshape(-1, width)
    gate_all = jnp.dot(held_rows, weight_gate, preferred_element_type=f32).reshape(
        experts, ticks, capacity, hidden_width
    )
    up_all = jnp.dot(held_rows, weight_up, preferred_element_type=f32).reshape(
        experts, ticks, capacity, hidden_width
    )
    hidden_all = (jax.nn.silu(gate_all) * up_all).astype(bf16)
    hidden_rows = hidden_all.reshape(-1, hidden_width)
    sum_gram = contract(hidden_rows, hidden_rows, 0, 0)
    trace_sum = jnp.trace(sum_gram)
    curvature = sum_gram * (hidden_width / (trace_sum + epsilon)) + damping * jnp.eye(
        hidden_width, dtype=f32
    )
    root = inverse_root(curvature, NS_ITERS)
    kept_g = jnp.zeros((experts, ticks, capacity, width), bf16)
    kept_gate = jnp.zeros((experts, ticks, capacity, hidden_width), bf16)
    kept_up = jnp.zeros((experts, ticks, capacity, hidden_width), bf16)
    total_steps = ticks + sections - 1
    for step_index in range(total_steps):
        offset = step_index - (sections - 1 - section)
        active = (offset >= 0) & (offset < ticks)
        micro = jnp.clip(offset, 0, ticks - 1)
        from_top = lax.dynamic_index_in_dim(cotangent, micro, 0, keepdims=False)
        current_cot = jnp.where(section == sections - 1, from_top, incoming)
        tick_scales = lax.dynamic_index_in_dim(scales_here, micro, 0, keepdims=False)
        scaled = (
            (tick_scales[:, :, None] * current_cot.astype(f32)[:, None, :])
            .astype(bf16)
            .reshape(2 * rows, width)
        )
        chosen = lax.dynamic_index_in_dim(tables[0], micro, 0, keepdims=False)
        send_scaled = jnp.einsum("nca,ad->ncd", chosen, scaled, preferred_element_type=f32).astype(
            bf16
        )
        got_scaled = lax.all_to_all(send_scaled, "expert", split_axis=0, concat_axis=0, tiled=True)
        gate = lax.dynamic_index_in_dim(gate_all, micro, 1, keepdims=False).reshape(
            -1, hidden_width
        )
        up_proj = lax.dynamic_index_in_dim(up_all, micro, 1, keepdims=False).reshape(
            -1, hidden_width
        )
        rows_g = got_scaled.reshape(-1, width)
        back_rows, d_gate, d_up = expert_backward(
            rows_g, gate, up_proj, weight_gate, weight_up, weight_down
        )

        def keep(kept, value):
            value = value.reshape(experts, capacity, -1)
            before = lax.dynamic_index_in_dim(kept, micro, 1, keepdims=False)
            return lax.dynamic_update_index_in_dim(
                kept, jnp.where(active, value, before), micro, 1
            )

        kept_g = keep(kept_g, rows_g)
        kept_gate = keep(kept_gate, d_gate)
        kept_up = keep(kept_up, d_up)
        came_back = lax.all_to_all(
            back_rows.reshape(experts, capacity, width),
            "expert",
            split_axis=0,
            concat_axis=0,
            tiled=True,
        )
        summed = (
            jnp.einsum("nca,ncd->ad", chosen, came_back, preferred_element_type=f32)
            .reshape(rows, 2, width)
            .sum(axis=1)
        )
        new_cot = (current_cot.astype(f32) + summed).astype(bf16)
        previous = lax.dynamic_index_in_dim(results, micro, 0, keepdims=False)
        results = lax.dynamic_update_index_in_dim(
            results, jnp.where(active, new_cot, previous), micro, 0
        )
        if step_index < total_steps - 1:
            incoming = from_behind(new_cot, "section", -1)
    sum_gate = contract(held_rows, kept_gate.reshape(-1, hidden_width), 0, 0)
    sum_up = contract(held_rows, kept_up.reshape(-1, hidden_width), 0, 0)
    sum_down = contract(hidden_rows, kept_g.reshape(-1, width), 0, 0)
    precond = jnp.dot(root.astype(bf16), sum_down.astype(bf16), preferred_element_type=f32)
    return (results[None], sum_gate[None, None], sum_up[None, None], precond[None, None])


def solution(mesh):
    return jax.shard_map(
        shards,
        mesh=mesh,
        in_specs=(
            P("section", None, "expert", None),
            P(None, "expert", None),
            P("section", None, "expert", None),
            P("section", None, "expert", None),
            P("section", "expert", None, None),
            P("section", "expert", None, None),
            P("section", "expert", None, None),
        ),
        out_specs=(
            P("section", None, "expert", None),
            P("section", "expert", None, None),
            P("section", "expert", None, None),
            P("section", "expert", None, None),
        ),
        check_vma=False,
    )
```

```python
import functools
import math

import jax
import jax.numpy as jnp
from jax import lax
from jax.experimental import pallas as pl
from jax.experimental.pallas import tpu as pltpu
from jax.sharding import PartitionSpec as P

NS_ITERS = 5


damping = 0.1
epsilon = 1e-06
MESH = pl.DeviceIdType.MESH


def silu_slope(values):
    logistic = jax.nn.sigmoid(values)
    return logistic * (1.0 + values * (1.0 - logistic))


def contract(former, latter, former_dim, latter_dim):
    return lax.dot_general(
        former,
        latter,
        (((former_dim,), (latter_dim,)), ((), ())),
        preferred_element_type=jnp.float32,
    )


def tick_tables(tick_ids, tick_scales, experts, capacity, pieces):
    rows = tick_ids.shape[0]
    flat_ids = tick_ids.reshape(-1)
    index = jnp.arange(flat_ids.shape[0], dtype=jnp.int32)
    earlier = (flat_ids[:, None] == flat_ids[None, :]) & (index[None, :] < index[:, None])
    ranking = jnp.sum(earlier.astype(jnp.int32), axis=1)
    target = flat_ids * capacity + ranking
    places = jnp.arange(experts * capacity, dtype=jnp.int32)
    chosen = places[:, None] == target[None, :]
    by_row = chosen.reshape(experts, capacity, rows, 2).any(axis=3)
    scale = jnp.sum(jnp.where(chosen, tick_scales.reshape(-1)[None, :], 0.0), axis=1)
    scale = jnp.broadcast_to(scale.reshape(experts, 1, capacity), (experts, pieces, capacity))
    same = jnp.eye(pieces, dtype=bool)
    packed = by_row[:, None, :, None, :] & same[None, :, None, :, None]
    packed = packed.reshape(experts * pieces * capacity, pieces * rows).astype(jnp.bfloat16)
    return packed, packed.T, scale.reshape(-1, 1)


def pipeline(
    experts, sections, ticks, pieces, block,
    x_ref, cot_ref, pick, pick_t, scale, spread, spread_t, wg, wu, wd,
    res, xs, gs, hid, dgate, dup, root,
    send_x, recv_x, send_g, recv_g, send_b, recv_b, hop, cur, gate, up, moving,
    sx, rx, sg, rg, sb, rb, sh, rh,
):
    f32, bf16 = jnp.float32, jnp.bfloat16
    me, sec = lax.axis_index("expert"), lax.axis_index("section")
    wide = x_ref.shape[2]
    top = sec == sections - 1

    barrier = pltpu.get_barrier_semaphore()

    @pl.loop(1, experts)
    def _(k):
        pl.semaphore_signal(
            barrier, inc=1, device_id={"expert": lax.rem(me + k, experts)}, device_id_type=MESH
        )

    @pl.when(sec > 0)
    def _():
        pl.semaphore_signal(barrier, inc=1, device_id={"section": sec - 1}, device_id_type=MESH)

    @pl.when(sec < sections - 1)
    def _():
        pl.semaphore_signal(barrier, inc=1, device_id={"section": sec + 1}, device_id_type=MESH)

    pl.semaphore_wait(
        barrier, experts - 1 + (sec > 0).astype(jnp.int32) + (sec < sections - 1).astype(jnp.int32)
    )

    def part(index):
        return pl.ds(pl.multiple_of(index * block, 16), block)

    def copy(send, recv, ssem, rsem, t, k, owner):
        peer = lax.rem(me + k, experts)
        return pltpu.make_async_remote_copy(
            src_ref=send.at[t, part(peer)],
            dst_ref=recv.at[t, part(owner)],
            send_sem=ssem.at[t, k],
            recv_sem=rsem.at[t, k],
            device_id={"expert": peer},
            device_id_type=MESH,
        )

    def start(send, recv, ssem, rsem, t):
        @pl.loop(1, experts)
        def _(k):
            copy(send, recv, ssem, rsem, t, k, me).start()

        recv[t, part(me)] = send[t, part(me)]

    def arrive(send, recv, ssem, rsem, t):
        @pl.loop(1, experts)
        def _(k):
            copy(send, recv, ssem, rsem, t, k, lax.rem(me - k + experts, experts)).wait_recv()

    ways_x = (send_x, recv_x, sx, rx)
    ways_g = (send_g, recv_g, sg, rg)
    ways_b = (send_b, recv_b, sb, rb)

    def columns(p):
        return pl.ds(p * wide, wide)

    def give_x(t):
        send_x[t] = contract(pick[t], x_ref[t], 1, 0).astype(bf16)
        start(*ways_x, t)

    def give_g(t, source):
        send_g[t] = (contract(pick[t], source, 1, 0) * scale[t]).astype(bf16)
        start(*ways_g, t)

    def forward(t):
        arrive(*ways_x, t)
        for p in range(pieces):
            xs[t, :, columns(p)] = contract(spread[p], recv_x[t], 1, 0).astype(bf16)
        rows_x = xs[t]
        gate[t] = contract(rows_x, wg[...], 1, 0)
        up[t] = contract(rows_x, wu[...], 1, 0)
        hid[t] = (jax.nn.silu(gate[t]) * up[t]).astype(bf16)

    def hop_copy(t):
        return pltpu.make_async_remote_copy(
            src_ref=res.at[t],
            dst_ref=hop.at[t],
            send_sem=sh.at[t],
            recv_sem=rh.at[t],
            device_id={"section": jnp.maximum(sec - 1, 0)},
            device_id_type=MESH,
        )

    def backward(t):
        arrive(*ways_g, t)
        for p in range(pieces):
            gs[t, :, columns(p)] = contract(spread[p], recv_g[t], 1, 0).astype(bf16)
        grad_hidden = contract(gs[t], wd[...], 1, 1)
        here, there = gate[t], up[t]
        dgate[t] = (grad_hidden * there * silu_slope(here)).astype(bf16)
        dup[t] = (grad_hidden * jax.nn.silu(here)).astype(bf16)
        total = None
        for p in range(pieces):
            back = contract(dgate[t], wg[columns(p), :], 1, 1) + contract(
                dup[t], wu[columns(p), :], 1, 1
            )
            term = contract(spread_t[p], back.astype(bf16), 1, 0)
            total = term if total is None else total + term
        send_b[t] = total.astype(bf16)
        start(*ways_b, t)

    def combine(t, source):
        arrive(*ways_b, t)
        res[t] = (source.astype(f32) + contract(pick_t[t], recv_b[t], 1, 0)).astype(bf16)

        @pl.when(sec > 0)
        def _():
            hop_copy(t).start()

    def inverse_root():
        size = moving.shape[0]
        eye = (
            lax.broadcasted_iota(jnp.int32, (size, size), 0)
            == lax.broadcasted_iota(jnp.int32, (size, size), 1)
        ).astype(f32)
        gram = contract(hid[0], hid[0], 0, 0)
        for t in range(1, ticks):
            gram = gram + contract(hid[t], hid[t], 0, 0)
        trace = jnp.sum(gram * eye, keepdims=True)
        curvature = gram * (size / (trace + epsilon)) + damping * eye
        norm = jnp.sqrt(jnp.sum(curvature * curvature, keepdims=True))
        moving[...] = curvature / norm
        root[...] = lax.rsqrt(jnp.sqrt(norm)) * (1.25 * eye - 0.25 * moving[...])

        def product(former, latter):
            return contract(former.astype(bf16), latter.astype(bf16), 1, 0)

        @pl.loop(1, NS_ITERS)
        def _(turn):
            current = moving[...]
            low = 0.0625 * product(current, current) - 0.625 * current
            high = 3.125 * low + product(low, low)
            moving[...] = 2.44140625 * current + product(high, current)
            held = root[...]
            root[...] = 1.25 * held - 0.25 * product(held, moving[...])

    give_x(0)

    @pl.when(top)
    def _():
        give_g(0, cot_ref[0])

    @pl.loop(1, ticks)
    def _(t):
        @pl.when(jnp.logical_not(top) | (t == 1))
        def _():
            give_x(t)

    @pl.when(jnp.logical_not(top))
    def _():
        @pl.loop(0, ticks)
        def _(t):
            forward(t)

        inverse_root()

    @pl.loop(0, ticks)
    def _(t):
        @pl.when(top)
        def _():
            cur[...] = cot_ref[t]
            forward(t)

        @pl.when(jnp.logical_not(top))
        def _():
            hop_copy(t).wait_recv()
            cur[...] = hop[t]
            give_g(t, cur[...])

        backward(t)

        @pl.when(top & (t + 1 < ticks))
        def _():
            give_g(t + 1, cot_ref[t + 1])

        @pl.when(top & (t + 2 < ticks))
        def _():
            give_x(t + 2)

        combine(t, cur[...])

    @pl.when(top)
    def _():
        inverse_root()

    @pl.loop(0, ticks)
    def _(t):
        @pl.loop(1, experts)
        def _(k):
            for ways in (ways_x, ways_g, ways_b):
                copy(*ways, t, k, me).wait_send()

        @pl.when(sec > 0)
        def _():
            hop_copy(t).wait_send()


def shards(section_inputs, cotangent, expert_ids, route_weights, w_gate, w_up, w_down):
    f32, bf16 = jnp.float32, jnp.bfloat16
    sections, experts = lax.axis_size("section"), lax.axis_size("expert")
    ticks, rows, width = section_inputs.shape[1:]
    capacity = max(2, 3 * rows // experts)
    pieces = 16 // math.gcd(capacity, 16)
    wide, block, slots = width // pieces, capacity * pieces, experts * capacity
    hidden_width = w_gate.shape[3]

    def packed(value):
        value = value.reshape(ticks, rows, pieces, wide)
        return jnp.swapaxes(value, 1, 2).reshape(ticks, pieces * rows, wide)

    pick, pick_t, scale = jax.vmap(
        lambda ids, scales: tick_tables(ids, scales, experts, capacity, pieces)
    )(expert_ids[0], route_weights[0])
    slot = jnp.arange(slots, dtype=jnp.int32)
    place = (slot // capacity) * block + slot % capacity
    place = place[None, :] + jnp.arange(pieces, dtype=jnp.int32)[:, None] * capacity
    spread = place[:, :, None] == jnp.arange(experts * block, dtype=jnp.int32)[None, None, :]
    spread = spread.astype(bf16)
    shape = jax.ShapeDtypeStruct
    travel = pltpu.VMEM((ticks, experts * block, wide), bf16)
    pair = pltpu.SemaphoreType.DMA((ticks, experts))
    vmem = pl.BlockSpec(memory_space=pltpu.VMEM)
    res, xs, gs, hid, dgate, dup, root = pl.pallas_call(
        functools.partial(pipeline, experts, sections, ticks, pieces, block),
        out_shape=[
            shape((ticks, pieces * rows, wide), bf16),
            shape((ticks, slots, width), bf16),
            shape((ticks, slots, width), bf16),
            shape((ticks, slots, hidden_width), bf16),
            shape((ticks, slots, hidden_width), bf16),
            shape((ticks, slots, hidden_width), bf16),
            shape((hidden_width, hidden_width), f32),
        ],
        in_specs=[vmem] * 10,
        out_specs=[vmem] * 7,
        scratch_shapes=[travel] * 6
        + [
            pltpu.VMEM((ticks, pieces * rows, wide), bf16),
            pltpu.VMEM((pieces * rows, wide), bf16),
            pltpu.VMEM((ticks, slots, hidden_width), f32),
            pltpu.VMEM((ticks, slots, hidden_width), f32),
            pltpu.VMEM((hidden_width, hidden_width), f32),
        ]
        + [pair] * 6
        + [pltpu.SemaphoreType.DMA((ticks,))] * 2,
        compiler_params=pltpu.CompilerParams(
            collective_id=0, has_side_effects=True, vmem_limit_bytes=60 * 1024 * 1024
        ),
    )(
        packed(section_inputs[0]), packed(cotangent), pick, pick_t, scale,
        spread, jnp.swapaxes(spread, 1, 2), w_gate[0, 0], w_up[0, 0], w_down[0, 0],
    )
    results = jnp.swapaxes(res.reshape(ticks, pieces, rows, wide), 1, 2).reshape(ticks, rows, width)
    xs, gs = xs.reshape(-1, width), gs.reshape(-1, width)
    hid, dgate, dup = (value.reshape(-1, hidden_width) for value in (hid, dgate, dup))
    sum_gate = contract(xs, dgate, 0, 0)
    sum_up = contract(xs, dup, 0, 0)
    sum_down = contract(hid, gs, 0, 0)
    precond = contract(root.astype(bf16), sum_down.astype(bf16), 1, 0)
    return (results[None], sum_gate[None, None], sum_up[None, None], precond[None, None])


def solution(mesh):
    return jax.shard_map(
        shards,
        mesh=mesh,
        in_specs=(
            P("section", None, "expert", None),
            P(None, "expert", None),
            P("section", None, "expert", None),
            P("section", None, "expert", None),
            P("section", "expert", None, None),
            P("section", "expert", None, None),
            P("section", "expert", None, None),
        ),
        out_specs=(
            P("section", None, "expert", None),
            P("section", "expert", None, None),
            P("section", "expert", None, None),
            P("section", "expert", None, None),
        ),
        check_vma=False,
    )
```
